128 devices in a mesh: dp: 2 (over z_hi), blk: 8 (over y, z_lo), seq: 8 (over x, core).
Axes of the slice: x: 4, y: 4, z: 4 (z_hi: 2, z_lo: 2; z = z_hi * 2 + z_lo), core: 2. Of those that a mesh axis runs over, the one named last changes fastest.
Arguments:
- inputs: bfloat16 [16384, 1024], P(('dp', 'blk', 'seq')), may hold values from -6 to 6
- cotangent: bfloat16 [16384, 1024], P(('dp', 'blk', 'seq')), may hold values from -6 to 6
- joint_weight: float32 [1024, 3072], P(('dp', 'seq')), may hold values from -0.1875 to 0.1875
- joint_first: float32 [1024, 3072], P(('dp', 'seq'))
- joint_second: float32 [1024, 3072], P(('dp', 'seq')), as said below
- dense_weight: float32 [1024, 1024], P(('dp', 'seq')), may hold values from -3.5 to 3.5
- dense_first: float32 [1024, 1024], P(('dp', 'seq'))
- dense_second: float32 [1024, 1024], P(('dp', 'seq')), as said below
- expand_weight: float32 [1024, 4096], P(('dp', 'seq')), may hold values from -0.1875 to 0.1875
- expand_first: float32 [1024, 4096], P(('dp', 'seq'))
- expand_second: float32 [1024, 4096], P(('dp', 'seq')), as said below
- shrink_weight: float32 [4096, 1024], P(('dp', 'seq')), may hold values from -0.09375 to 0.09375
- shrink_first: float32 [4096, 1024], P(('dp', 'seq'))
- shrink_second: float32 [4096, 1024], P(('dp', 'seq')), as said below
- vectors: float32 [1024, 13], P(('dp', 'seq')), as said below
- vectors_first: float32 [1024, 13], P(('dp', 'seq'))
- vectors_second: float32 [1024, 13], P(('dp', 'seq')), as said below
Outputs:
- output: bfloat16 [16384, 1024], P(('dp', 'blk', 'seq'))
- input_grad: float32 [16384, 1024], P(('dp', 'blk', 'seq'))
- joint_first_new: float32 [1024, 3072], P(('dp', 'seq'))
- joint_second_new: float32 [1024, 3072], P(('dp', 'seq'))
- joint_weight_new: float32 [1024, 3072], P(('dp', 'seq'))
- dense_first_new: float32 [1024, 1024], P(('dp', 'seq'))
- dense_second_new: float32 [1024, 1024], P(('dp', 'seq'))
- dense_weight_new: float32 [1024, 1024], P(('dp', 'seq'))
- expand_first_new: float32 [1024, 4096], P(('dp', 'seq'))
- expand_second_new: float32 [1024, 4096], P(('dp', 'seq'))
- expand_weight_new: float32 [1024, 4096], P(('dp', 'seq'))
- shrink_first_new: float32 [4096, 1024], P(('dp', 'seq'))
- shrink_second_new: float32 [4096, 1024], P(('dp', 'seq'))
- shrink_weight_new: float32 [4096, 1024], P(('dp', 'seq'))
- vectors_first_new: float32 [1024, 13], P(('dp', 'seq'))
- vectors_second_new: float32 [1024, 13], P(('dp', 'seq'))
- vectors_new: float32 [1024, 13], P(('dp', 'seq'))
The draws below stay inside these ranges and needn't reach their ends.
Inputs may be any that keep to these rules, and one draw needn't show every extreme that they name: `vectors`: gains of the two norms lie in [0.7, 1.3], biases in [-0.8, 0.8]. `joint_second`: positive. `dense_second`: positive. `expand_second`: positive. `shrink_second`: positive. `vectors_second`: positive.
All inputs are finite; a program needn't handle non-finite values.
Results may differ from the reference program's by a relative error of at most 0.028.
Values may be sent and summed in bfloat16 or wider, within the bound.
A program may use at most 192 MiB of HBM per device.

```python
import math
from functools import partial
import jax
import jax.numpy as jnp
from jax import lax

D = 1024
HEADS = 16
HEAD_DIM = 64
ROT = 16
FF = 4096
STEP = 10
SEQS = 2
LENGTH = 8192
TOKENS = 16384
VCOLS = 13


def first_moment(key, array_shape, spread):
    return 0.1 / 0.9 * spread * jax.random.truncated_normal(key, -4.0, 4.0, array_shape, jnp.float32)


def second_moment(key, array_shape, spread):
    factor = jnp.exp(jax.random.uniform(key, array_shape, jnp.float32, math.log(0.5), math.log(2.0)))
    return 0.05 / 0.95 * 2.0 * spread * spread * factor


def draw_vectors(key, part):
    key = jax.random.fold_in(key, 1)
    gain_key, bias_key = jax.random.split(key)
    column = jnp.broadcast_to(jnp.arange(VCOLS)[None, :], (D, VCOLS))
    is_gain = (column == 0) | (column == 2)
    gain_values = jax.random.uniform(gain_key, (D, VCOLS), jnp.float32, 0.7, 1.3)
    biases = 0.2 * jax.random.truncated_normal(bias_key, -4.0, 4.0, (D, VCOLS), jnp.float32)
    return jnp.where(is_gain, gain_values, biases)


def draw_joint_first(key, part):
    key = jax.random.fold_in(key, 11)
    return first_moment(key, (D, 3 * D), math.sqrt(TOKENS))


def draw_joint_second(key, part):
    key = jax.random.fold_in(key, 12)
    return second_moment(key, (D, 3 * D), math.sqrt(TOKENS))


def draw_dense_first(key, part):
    key = jax.random.fold_in(key, 21)
    return first_moment(key, (D, D), 4.0 * math.sqrt(TOKENS / LENGTH))


def draw_dense_second(key, part):
    key = jax.random.fold_in(key, 22)
    return second_moment(key, (D, D), 4.0 * math.sqrt(TOKENS / LENGTH))


def draw_expand_first(key, part):
    key = jax.random.fold_in(key, 31)
    return first_moment(key, (D, FF), 0.3 * math.sqrt(TOKENS))


def draw_expand_second(key, part):
    key = jax.random.fold_in(key, 32)
    return second_moment(key, (D, FF), 0.3 * math.sqrt(TOKENS))


def draw_shrink_first(key, part):
    key = jax.random.fold_in(key, 41)
    return first_moment(key, (FF, D), 0.65 * math.sqrt(TOKENS))


def draw_shrink_second(key, part):
    key = jax.random.fold_in(key, 42)
    return second_moment(key, (FF, D), 0.65 * math.sqrt(TOKENS))


def draw_vectors_first(key, part):
    key = jax.random.fold_in(key, 51)
    return first_moment(key, (D, VCOLS), math.sqrt(TOKENS))


def draw_vectors_second(key, part):
    key = jax.random.fold_in(key, 52)
    return second_moment(key, (D, VCOLS), math.sqrt(TOKENS))


def block_levels(stream_key, extent, cuts, low, top_value):
    factor_of = 1.0
    for position, blocks in cuts:
        draws = jax.random.uniform(jax.random.fold_in(jax.random.fold_in(stream_key, 6), position), (blocks,), jnp.float32, low / len(cuts), top_value / len(cuts))
        factor_of = factor_of * jnp.repeat(jnp.exp(draws), extent[position] // blocks).reshape((-1,) + (1,) * (len(extent) - 1 - position))
    return factor_of


def scatter_about(stream_key, extent, width, reach, cuts=(), kind=jnp.bfloat16):
    array = width * jax.random.normal(stream_key, extent, jnp.float32)
    if cuts:
        array = array * block_levels(stream_key, extent, cuts, -0.22, 0.18)
    return jnp.clip(array, -reach, reach).astype(kind)


def setup_inputs(seed: int = 0) -> dict:
    arg_keys = jax.random.split(jax.random.key(seed), 18)
    inputs = scatter_about(arg_keys[0], (TOKENS, D), 1.0, 6.0, ((0, 128),))
    cotangent = scatter_about(arg_keys[1], (TOKENS, D), 1.0, 6.0, ((0, 128),))
    joint_weight = scatter_about(arg_keys[2], (D, 3 * D), D ** -0.5, 0.1875, ((0, 16),), jnp.float32)
    joint_first = draw_joint_first(jax.random.fold_in(arg_keys[17], 71), 0)
    joint_second = draw_joint_second(jax.random.fold_in(arg_keys[17], 71), 0)
    dense_weight = scatter_about(arg_keys[5], (D, D), (max(1, 24 * D // LENGTH)) ** -0.5, 3.5, ((0, 16),), jnp.float32)
    dense_first = draw_dense_first(jax.random.fold_in(arg_keys[17], 71), 0)
    dense_second = draw_dense_second(jax.random.fold_in(arg_keys[17], 71), 0)
    expand_weight = scatter_about(arg_keys[8], (D, FF), D ** -0.5, 0.1875, ((0, 16),), jnp.float32)
    expand_first = draw_expand_first(jax.random.fold_in(arg_keys[17], 71), 0)
    expand_second = draw_expand_second(jax.random.fold_in(arg_keys[17], 71), 0)
    shrink_weight = scatter_about(arg_keys[11], (FF, D), FF ** -0.5, 0.09375, ((0, 16),), jnp.float32)
    shrink_first = draw_shrink_first(jax.random.fold_in(arg_keys[17], 71), 0)
    shrink_second = draw_shrink_second(jax.random.fold_in(arg_keys[17], 71), 0)
    vectors = draw_vectors(jax.random.fold_in(arg_keys[17], 71), 0)
    vectors_first = draw_vectors_first(jax.random.fold_in(arg_keys[17], 71), 0)
    vectors_second = draw_vectors_second(jax.random.fold_in(arg_keys[17], 71), 0)
    return dict(inputs=inputs, cotangent=cotangent, joint_weight=joint_weight, joint_first=joint_first, joint_second=joint_second, dense_weight=dense_weight, dense_first=dense_first, dense_second=dense_second, expand_weight=expand_weight, expand_first=expand_first, expand_second=expand_second, shrink_weight=shrink_weight, shrink_first=shrink_first, shrink_second=shrink_second, vectors=vectors, vectors_first=vectors_first, vectors_second=vectors_second)


@jax.custom_vjp
def low(v):
    return lax.optimization_barrier(v.astype(jnp.bfloat16)).astype(jnp.float32)

@jax.custom_vjp
def low_back(v):
    return v

def low_keep(v):
    return (low(v), None)

def low_pass(kept, grad):
    return (grad,)

def back_keep(v):
    return (v, None)

def back_low(kept, grad):
    return (low(grad),)
low.defvjp(low_keep, low_pass)
low_back.defvjp(back_keep, back_low)
eps_norm = 1e-05
beta_one = 0.9
beta_two = 0.95
adam_eps = 1e-08
weight_decay = 0.01
masked_score = -1e+30

def matmul(left_side, right_side):
    return jnp.dot(left_side, right_side, precision=lax.Precision.HIGHEST, preferred_element_type=jnp.float32)

def layer_norm(inputs, gain_vec, shift_vec):
    mean_value = lax.optimization_barrier(jnp.mean(inputs, axis=-1, keepdims=True))
    centred = inputs - mean_value
    inv_std = lax.rsqrt(lax.optimization_barrier(jnp.mean(centred * centred, axis=-1, keepdims=True)) + eps_norm)
    return centred * inv_std * gain_vec + shift_vec

def rotate(field_in, positions):
    half_dims = ROT // 2
    freqs = jnp.power(10000.0, -2.0 * jnp.arange(half_dims).astype(jnp.float32) / ROT)
    angles = positions.astype(jnp.float32)[:, None] * freqs[None, :]
    cosine = jnp.cos(angles)[:, None, :]
    sine = jnp.sin(angles)[:, None, :]
    lower = field_in[..., :half_dims]
    upper = field_in[..., half_dims:ROT]
    return jnp.concatenate([lower * cosine - upper * sine, upper * cosine + lower * sine, field_in[..., ROT:]], axis=-1)

def attend_head(offset, operands):
    query_rows, key_rows, value_rows = operands
    scores = low_back(matmul(query_rows, key_rows.T) * HEAD_DIM ** (-0.5))
    query_pos = offset + jnp.arange(query_rows.shape[0])
    key_pos = jnp.arange(key_rows.shape[0])
    scores = jnp.where(key_pos[None, :] <= query_pos[:, None], scores, masked_score)
    attn_probs = jax.nn.softmax(scores, axis=-1)
    return low(low_back(matmul(low(attn_probs), value_rows)))

def attention(query_rows, key_rows, value_rows):
    query_heads = jnp.transpose(query_rows, (1, 0, 2))
    key_heads = jnp.transpose(key_rows, (1, 0, 2))
    value_heads = jnp.transpose(value_rows, (1, 0, 2))
    block_size = min(1024, LENGTH)
    pieces = []
    for block_index in range(LENGTH // block_size):
        begin = block_index * block_size
        limit = begin + block_size
        piece = lax.map(jax.checkpoint(partial(attend_head, begin)), (query_heads[:, begin:limit], key_heads[:, :limit], value_heads[:, :limit]))
        pieces.append(piece)
    joined = jnp.concatenate(pieces, axis=1)
    return jnp.transpose(joined, (1, 0, 2)).reshape(LENGTH, D)

def forward(inputs, joint_weight, dense_weight, expand_weight, shrink_weight, vectors):
    joint_low = low(joint_weight)
    dense_low = low(dense_weight)
    expand_low = low(expand_weight)
    shrink_low = low(shrink_weight)
    vector_low = low(vectors)
    gain_one = vector_low[:, 0]
    shift_one = vector_low[:, 1]
    gain_two = vector_low[:, 2]
    shift_two = vector_low[:, 3]
    bias_joint = vector_low[:, 4:7].T.reshape(3 * D)
    bias_dense = vector_low[:, 7]
    bias_shrink = vector_low[:, 8]
    bias_expand = vector_low[:, 9:].reshape(FF)
    normed_one = low(layer_norm(inputs, gain_one, shift_one))
    triple = low(low_back(matmul(normed_one, joint_low) + bias_joint))
    queries = triple[:, 0:D].reshape(SEQS, LENGTH, HEADS, HEAD_DIM)
    key_part = triple[:, D:2 * D].reshape(SEQS, LENGTH, HEADS, HEAD_DIM)
    value_part = triple[:, 2 * D:3 * D].reshape(SEQS, LENGTH, HEADS, HEAD_DIM)
    positions = jnp.arange(LENGTH)
    rotated_q = low(rotate(queries, positions))
    rotated_k = low(rotate(key_part, positions))
    attended = jnp.concatenate([attention(rotated_q[sequence], rotated_k[sequence], value_part[sequence]) for sequence in range(SEQS)], axis=0)
    attn_out = matmul(attended, dense_low) + bias_dense
    normed_two = low(layer_norm(inputs, gain_two, shift_two))
    hidden_pre = low_back(matmul(normed_two, expand_low) + bias_expand)
    activated = low(jax.nn.gelu(hidden_pre, approximate=False))
    mlp_out = matmul(activated, shrink_low) + bias_shrink
    return inputs + attn_out + mlp_out

def adam_update(grad_in, first_old, second_old, master, rate, decay_rate):
    first_new = beta_one * first_old + (1.0 - beta_one) * grad_in
    second_new = beta_two * second_old + (1.0 - beta_two) * grad_in * grad_in
    root_second = jnp.sqrt(second_new / (1.0 - beta_two ** STEP)) + adam_eps
    master_new = master * (1.0 - rate * decay_rate) - rate * (first_new / (1.0 - beta_one ** STEP)) / root_second
    return (first_new, second_new, master_new)

def reference(inputs, cotangent, joint_weight, joint_first, joint_second, dense_weight, dense_first, dense_second, expand_weight, expand_first, expand_second, shrink_weight, shrink_first, shrink_second, vectors, vectors_first, vectors_second):
    result, pullback = jax.vjp(forward, inputs.astype(jnp.float32), joint_weight, dense_weight, expand_weight, shrink_weight, vectors)
    grad_input, grad_joint, grad_dense, grad_expand, grad_shrink, grad_vectors = pullback(cotangent.astype(jnp.float32))
    joint_m, joint_v, joint_w = adam_update(grad_joint, joint_first, joint_second, joint_weight, 0.1, weight_decay)
    dense_m, dense_v, dense_w = adam_update(grad_dense, dense_first, dense_second, dense_weight, 1.0, weight_decay)
    expand_m, expand_v, expand_w = adam_update(grad_expand, expand_first, expand_second, expand_weight, 0.1, weight_decay)
    shrink_m, shrink_v, shrink_w = adam_update(grad_shrink, shrink_first, shrink_second, shrink_weight, 0.05, weight_decay)
    vector_m, vector_v, vector_w = adam_update(grad_vectors, vectors_first, vectors_second, vectors, 1.0, 0.0)
    return (result.astype(jnp.bfloat16), grad_input, joint_m, joint_v, joint_w, dense_m, dense_v, dense_w, expand_m, expand_v, expand_w, shrink_m, shrink_v, shrink_w, vector_m, vector_v, vector_w)
```

```python
from functools import partial

import jax
import jax.numpy as jnp
from jax import lax
from jax.experimental import pallas as pl
from jax.experimental.pallas import tpu as pltpu
from jax.sharding import PartitionSpec as P

D = 1024
HEADS = 16
HEAD_DIM = 64
ROT = 16
FF = 4096
STEP = 10
VCOLS = 13
DP = 2
BLK = 8
SEQ = 8
OWN = 16
ROWS = 128
HALF = 512
BLOCK = 1024
LAST = 15

eps_norm = 1e-05
beta_one = 0.9
beta_two = 0.95
adam_eps = 1e-08
weight_decay = 0.01
masked_score = -1e30

bf16 = jnp.bfloat16
f32 = jnp.float32
MESH = pl.DeviceIdType.MESH
ANY = pl.BlockSpec(memory_space=pl.ANY)
VMEM = pl.BlockSpec(memory_space=pltpu.VMEM)
DMA = pltpu.SemaphoreType.DMA


def remote(src, dst, send_sem, recv_sem, device):
    return pltpu.make_async_remote_copy(
        src_ref=src,
        dst_ref=dst,
        send_sem=send_sem,
        recv_sem=recv_sem,
        device_id=device,
        device_id_type=MESH,
    )


def loop(begin, end, body):
    def step(index, unused):
        body(index)
        return unused

    lax.fori_loop(begin, end, step, jnp.int32(0))


def place():
    return lax.axis_index("dp"), lax.axis_index("blk"), lax.axis_index("seq")


def ring(s):
    return (s + 2) % SEQ, (s + 6) % SEQ, (s + 4) % SEQ, s + 1 - 2 * (s % 2)


def gather_kernel(
    x, c, wj, we, ws, wd, vec, X, C, WJ, WE, WS, WD, VEC, xs, xr, ws_s, ws_r, ds, dr, loc
):
    dp, g, s = place()
    me = dp * SEQ + s
    beside = g + 1 - 2 * (g % 2)

    def peer(p):
        return p // SEQ, jnp.where(p // SEQ == dp, g, beside), p % SEQ

    right, left, across, sibling = ring(s)
    barrier = pltpu.get_barrier_semaphore()

    def greet_peer(t):
        p = (me + t) % OWN
        pl.semaphore_signal(barrier, inc=1, device_id=peer(p), device_id_type=MESH)

    loop(1, OWN, greet_peer)
    pl.semaphore_wait(barrier, OWN - 1)

    def pass_on(source, whole, array, slot, number, target):
        return remote(
            source, whole.at[slot], xs.at[number], xr.at[array, slot], (dp, g, target)
        )

    def first_copies():
        return (
            pass_on(x, X, 0, s, 0, right),
            pass_on(c, C, 1, s, 1, left),
            pass_on(c, C, 1, s, 2, right),
            pass_on(x, X, 0, s, 3, left),
            pass_on(x, X, 0, s, 4, sibling),
            pass_on(c, C, 1, s, 5, sibling),
        )

    def relays():
        return (
            pass_on(X.at[left], X, 0, left, 6, right),
            pass_on(C.at[right], C, 1, right, 7, left),
            pass_on(X.at[left], X, 0, left, 8, sibling),
            pass_on(C.at[right], C, 1, right, 9, sibling),
            pass_on(C.at[left], C, 1, left, 10, sibling),
            pass_on(X.at[right], X, 0, right, 11, sibling),
            pass_on(X.at[across], X, 0, across, 12, sibling),
            pass_on(C.at[across], C, 1, across, 13, sibling),
        )

    def arrive(array, slot):
        source, whole = ((x, X), (c, C))[array]
        pass_on(source, whole, array, slot, 0, sibling).wait_recv()

    def weight_copies(t):
        p = (me + t) % OWN
        target = peer(p)
        return (
            remote(wj.at[p % SEQ], WJ.at[me], ws_s.at[0, t], ws_r.at[0, me], target),
            remote(vec, VEC.at[me], ws_s.at[1, t], ws_r.at[1, me], target),
        )

    def pair_copies():
        target = (1 - dp, beside, s)
        return (
            remote(ws, WS.at[dp], ds.at[0], dr.at[0], target),
            remote(wd, WD.at[dp], ds.at[1], dr.at[1], target),
            remote(we, WE.at[dp], ds.at[2], dr.at[2], target),
        )

    def start_weights(t):
        for copy in weight_copies(t):
            copy.start()

    local = (
        pltpu.make_async_copy(wj.at[s], WJ.at[me], loc.at[0]),
        pltpu.make_async_copy(we, WE.at[dp], loc.at[1]),
        pltpu.make_async_copy(vec, VEC.at[me], loc.at[2]),
        pltpu.make_async_copy(ws, WS.at[dp], loc.at[3]),
        pltpu.make_async_copy(wd, WD.at[dp], loc.at[4]),
        pltpu.make_async_copy(x, X.at[s], loc.at[5]),
        pltpu.make_async_copy(c, C.at[s], loc.at[6]),
    )
    for copy in first_copies():
        copy.start()
    for copy in pair_copies():
        copy.start()
    loop(1, OWN, start_weights)
    for copy in local:
        copy.start()
    relayed = relays()
    arrive(0, left)
    relayed[0].start()
    relayed[2].start()
    arrive(1, right)
    relayed[1].start()
    relayed[3].start()
    arrive(1, left)
    relayed[4].start()
    arrive(0, right)
    relayed[5].start()
    arrive(0, across)
    relayed[6].start()
    arrive(1, across)
    relayed[7].start()
    for copy in local:
        copy.wait()
    for shift in range(0, 8, 2):
        for array in range(2):
            arrive(array, (sibling + shift) % SEQ)

    def take_weight(t):
        p = (me + t) % OWN
        target = peer(p)
        remote(wj.at[0], WJ.at[p], ws_s.at[0, t], ws_r.at[0, p], target).wait_recv()
        remote(vec, VEC.at[p], ws_s.at[1, t], ws_r.at[1, p], target).wait_recv()
        for copy in weight_copies(t):
            copy.wait_send()

    loop(1, OWN, take_weight)
    target = (1 - dp, beside, s)
    remote(ws, WS.at[1 - dp], ds.at[0], dr.at[0], target).wait_recv()
    remote(wd, WD.at[1 - dp], ds.at[1], dr.at[1], target).wait_recv()
    remote(we, WE.at[1 - dp], ds.at[2], dr.at[2], target).wait_recv()
    for copy in first_copies() + relayed + pair_copies():
        copy.wait_send()


def gather(x, c, wj, we, ws, wd, vec):
    def shape(*dims):
        return jax.ShapeDtypeStruct(dims, bf16)

    return pl.pallas_call(
        gather_kernel,
        out_shape=(
            shape(8, ROWS, D),
            shape(8, ROWS, D),
            shape(OWN, 64, 384),
            shape(2, SEQ, 64, 512),
            shape(2, 256, D),
            shape(2, 64, D),
            shape(OWN, 16, 128),
        ),
        in_specs=[ANY] * 7,
        out_specs=(ANY,) * 7,
        scratch_shapes=[
            DMA((14,)),
            DMA((2, 8)),
            DMA((2, OWN)),
            DMA((2, OWN)),
            DMA((3,)),
            DMA((3,)),
            DMA((7,)),
        ],
        compiler_params=pltpu.CompilerParams(collective_id=0, has_side_effects=True),
        name="gather_tokens_weights",
    )(x, c, wj, we, ws, wd, vec)


NT = (((1,), (1,)), ((), ()))
NN = (((1,), (0,)), ((), ()))


def dot(left, right, dims):
    return lax.dot_general(left, right, dims, preferred_element_type=f32)


def low_half(g):
    return jnp.where(g < BLK // 2, 2 * g, LAST - 2 * g)


def attention_kernel(
    q, do, kv, mask, we,
    att, dq, dkv, WE,
    kvall, qs, dos, q2, do2, top, total, acc, lse, delta, dq_acc, stage, sbuf, rbuf, relay,
    att_out, att_in, dq_out, dq_in,
    ks, kr, bs, br, fs, ls, lr, wsend, wrecv, psend, precv, loc,
):
    dp, g, s = place()
    low = low_half(g)
    keep = jnp.where(g < BLK // 2, 0, 1)
    given = 1 - keep
    partner = (dp, BLK - 1 - g, s)
    barrier = pltpu.get_barrier_semaphore()

    def greet(t):
        pl.semaphore_signal(
            barrier, inc=1, device_id=(dp, (g + t) % BLK, s), device_id_type=MESH
        )

    def greet_row(t):
        pl.semaphore_signal(
            barrier, inc=1, device_id=(dp, g, (s + t) % SEQ), device_id_type=MESH
        )

    loop(1, BLK, greet)
    loop(1, SEQ, greet_row)
    pl.semaphore_wait(barrier, BLK + SEQ - 2)

    def swap(number, source, target):
        return remote(source, target, psend.at[number], precv.at[number], partner)

    swap(0, q.at[1], qs.at[keep]).start()
    y, zl = g // 2, g % 2

    def at(dy, z):
        return (y + dy) % 4 * 2 + z

    def order(t):
        k = t // 2
        return jnp.where(k == 2, 3, jnp.where(k == 3, 2, k)), t % 2

    def need(p, j):
        return j <= LAST - low_half(p)

    def send_kv(p, half):
        j = 2 * g + half
        return remote(kv.at[half], kvall.at[j], ks.at[p, half], kr.at[j], (dp, p, s))

    def each_kv(act):
        def step(u):
            dy, dz = order(u // 2 + 1)
            half = u % 2
            z = (zl + dz) % 2
            p, beyond = at(dy, z), at(2, z)
            j = 2 * g + half
            passes = jnp.logical_or(
                jnp.logical_and(dy == 1, half == 0), jnp.logical_and(dy == 3, half == 1)
            )

            @pl.when(jnp.logical_or(need(p, j), jnp.logical_and(passes, need(beyond, j))))
            def _():
                act(send_kv(p, half))

        loop(0, 2 * 5, step)

    def pass_kv(j, half, z, p):
        return remote(
            kvall.at[j], kvall.at[j], fs.at[half, z], kr.at[j], (dp, p, s)
        )

    each_kv(lambda copy: copy.start())
    swap(1, do.at[1], dos.at[keep]).start()
    kvall[2 * g] = kv[0]
    kvall[2 * g + 1] = kv[1]
    qs[keep] = q[0]
    dos[keep] = do[0]

    def weight_copies(t):
        target = (s + t) % SEQ
        return tuple(
            remote(
                we.at[d, target], WE.at[d * SEQ + s], wsend.at[d, t], wrecv.at[d, s], (dp, g, target)
            )
            for d in range(2)
        )

    def start_weights(t):
        for copy in weight_copies(t):
            copy.start()

    local = tuple(
        pltpu.make_async_copy(we.at[d, s], WE.at[d * SEQ + s], loc.at[d]) for d in range(2)
    )
    loop(1, SEQ, start_weights)
    for copy in local:
        copy.start()

    top[...] = jnp.full(top.shape, masked_score, f32)
    total[...] = jnp.zeros(total.shape, f32)
    acc[...] = jnp.zeros(acc.shape, f32)
    dq_acc[...] = jnp.zeros(dq_acc.shape, f32)
    dkv[...] = jnp.zeros(dkv.shape, f32)

    def allowed():
        key_row = lax.broadcasted_iota(jnp.int32, (HALF, HALF), 0)
        query_row = lax.broadcasted_iota(jnp.int32, (HALF, HALF), 1)
        return key_row <= query_row

    swap(0, q.at[1], qs.at[given]).wait_recv()
    for slot in range(2):
        for h in range(2):
            q2[h, slot] = qs[slot] * mask[h]

    def forward_pair(slot, j, diagonal):
        keys = kvall[j, :, 0:128]
        values_t = kvall[j, :, 128:256].T
        for h in range(2):
            scores = dot(keys, q2[h, slot], NT)
            if diagonal:
                scores = jnp.where(allowed(), scores, masked_score)
            old = top[slot, h]
            new = jnp.maximum(old, jnp.max(scores, axis=0, keepdims=True))
            terms = jnp.exp(scores - new)
            factor = jnp.exp(old - new)
            top[slot, h] = new
            total[slot, h] = total[slot, h] * factor + jnp.sum(terms, axis=0, keepdims=True)
            acc[slot, h] = acc[slot, h] * factor + dot(
                values_t[64 * h : 64 * h + 64], terms.astype(bf16), NN
            )

    def both_kinds(pair, slot, j):
        mine = jnp.where(slot == 0, low, LAST - low)

        @pl.when(j < mine)
        def _():
            pair(slot, j, False)

        @pl.when(j == mine)
        def _():
            pair(slot, j, True)

    def passing(dy, half):
        passes = jnp.logical_or(
            jnp.logical_and(dy == 3, half == 0), jnp.logical_and(dy == 1, half == 1)
        )
        return passes, at(jnp.where(half == 0, 1, 3), zl)

    def forward_keys(u):
        dy, dz = order(u // 2)
        half = u % 2
        z = (zl + dz) % 2
        p = at(dy, z)
        j = 2 * p + half
        passes, beyond = passing(dy, half)
        passes = jnp.logical_and(passes, need(beyond, j))

        @pl.when(jnp.logical_and(u >= 2, jnp.logical_or(need(g, j), passes)))
        def _():
            remote(
                kv.at[0], kvall.at[j], ks.at[p, 0], kr.at[j], (dp, p, s)
            ).wait_recv()

        @pl.when(passes)
        def _():
            pass_kv(j, half, z, beyond).start()

        loop(0, 2, lambda slot: both_kinds(forward_pair, slot, j))

    loop(0, 2 * BLK, forward_keys)

    swap(1, do.at[1], dos.at[given]).wait_recv()
    for slot in range(2):
        grads_t = dos[slot].T.astype(f32)
        for h in range(2):
            do2[h, slot] = dos[slot] * mask[h]
            rows = acc[slot, h] / total[slot, h]
            part = slice(64 * h, 64 * h + 64)
            att_out[slot, part] = rows.astype(bf16)
            lse[slot, h] = top[slot, h] + jnp.log(total[slot, h])
            delta[slot, h] = jnp.sum(rows * grads_t[part], axis=0, keepdims=True)
    swap(2, att_out.at[given], att_in).start()
    att[:, 0:HALF] = att_out[keep]

    def backward_pair(slot, j, diagonal):
        keys = kvall[j, :, 0:128]
        values = kvall[j, :, 128:256]
        keys_t = keys.T
        for h in range(2):
            queries = q2[h, slot]
            grads = do2[h, slot]
            scores = dot(keys, queries, NT)
            probs = jnp.exp(scores - lse[slot, h])
            if diagonal:
                probs = jnp.where(allowed(), probs, 0.0)
            grad_probs = dot(values, grads, NT)
            grad_scores = (probs * (grad_probs - delta[slot, h])).astype(bf16)
            stage[:, 128:256] += dot(probs.astype(bf16), grads, NN)
            stage[:, 0:128] += dot(grad_scores, queries, NN)
            dq_acc[slot, h] += dot(keys_t[64 * h : 64 * h + 64], grad_scores, NN)

    def send_back(p, j):
        return remote(
            sbuf.at[j], rbuf.at[g, j % 2], bs.at[j], br.at[g, j % 2], (dp, p, s)
        )

    def step_of(t):
        dy, dz = order(7 - t)
        return dy, (zl + dz) % 2

    def send_far(p, j):
        half = j % 2
        through = at(jnp.where(half == 0, 1, 3), p % 2)
        return remote(
            sbuf.at[j], relay.at[half, zl], bs.at[j], lr.at[half, zl], (dp, through, s)
        )

    def pass_back(half, z):
        source = at(jnp.where(half == 0, 3, 1), z)
        p = at(jnp.where(half == 0, 1, 3), zl)
        copy = remote(
            relay.at[half, z], rbuf.at[source, half], ls.at[half, z], br.at[source, half], (dp, p, s)
        )
        return need(source, 2 * p + half), copy

    def each_pass(act):
        def step(i):
            there, copy = pass_back(i // 2, i % 2)

            @pl.when(there)
            def _():
                act(i // 2, i % 2, copy)

        loop(0, 4, step)

    def start_pass(half, z, copy):
        remote(
            sbuf.at[0], relay.at[half, z], bs.at[0], lr.at[half, z], (dp, at(2 * half + 1, z), s)
        ).wait_recv()
        copy.start()

    def backward_keys(u):
        dy, z = step_of(u // 2)
        p = at(dy, z)
        j = 2 * p + u % 2

        @pl.when(u == 10)
        def _():
            each_pass(start_pass)

        @pl.when(j <= LAST - low)
        def _():
            stage[...] = jnp.zeros(stage.shape, f32)
            loop(0, 2, lambda slot: both_kinds(backward_pair, slot, j))

            @pl.when(p != g)
            def _():
                sbuf[j] = stage[...].astype(bf16)

            @pl.when(jnp.logical_and(p != g, dy != 2))
            def _():
                send_back(p, j).start()

            @pl.when(dy == 2)
            def _():
                send_far(p, j).start()

            @pl.when(p == g)
            def _():
                dkv[u % 2] = stage[...]

    loop(0, 2 * BLK, backward_keys)

    scale = HEAD_DIM ** (-0.5)
    for slot in range(2):
        for h in range(2):
            dq_out[slot, 64 * h : 64 * h + 64] = (dq_acc[slot, h] * scale).astype(bf16)
    swap(3, dq_out.at[given], dq_in).start()
    dq[0] = dq_acc[keep].reshape(128, HALF).T * scale

    def take_back(u):
        p = (g + 1 + u // 2) % BLK
        half = u % 2

        @pl.when(2 * g + half <= LAST - low_half(p))
        def _():
            remote(
                sbuf.at[0], rbuf.at[p, half], bs.at[0], br.at[p, half], (dp, p, s)
            ).wait_recv()
            dkv[half] += rbuf[p, half].astype(f32)

    loop(0, 2 * (BLK - 1), take_back)
    each_kv(lambda copy: copy.wait_send())

    each_pass(lambda half, z, copy: copy.wait_send())

    def sent(u):
        dy, z = step_of(u // 2)
        p = at(dy, z)
        j = 2 * p + u % 2

        @pl.when(need(g, j))
        def _():
            send_back(p, j).wait_send()

    def sent_pass(u):
        dy, dz = order(u // 2)
        half = u % 2
        z = (zl + dz) % 2
        j = 2 * at(dy, z) + half
        passes, beyond = passing(dy, half)

        @pl.when(jnp.logical_and(passes, need(beyond, j)))
        def _():
            pass_kv(j, half, z, beyond).wait_send()

    loop(4, 12, sent_pass)
    loop(0, 2 * (BLK - 1), sent)
    for copy in local:
        copy.wait()

    def take_weights(t):
        source = (s + t) % SEQ
        for d in range(2):
            remote(
                we.at[d, 0], WE.at[d * SEQ + source], wsend.at[d, t], wrecv.at[d, source], (dp, g, source)
            ).wait_recv()
        for copy in weight_copies(t):
            copy.wait_send()

    loop(1, SEQ, take_weights)
    swap(2, att_out.at[given], att_in).wait_recv()
    swap(3, dq_out.at[given], dq_in).wait_recv()
    att[:, HALF:BLOCK] = att_in[...]
    dq[1] = dq_in[...].astype(f32).T
    swap(0, q.at[1], qs.at[keep]).wait_send()
    swap(1, do.at[1], dos.at[keep]).wait_send()
    swap(2, att_out.at[given], att_in).wait_send()
    swap(3, dq_out.at[given], dq_in).wait_send()


def attention(q, do, kv, mask, we):
    return pl.pallas_call(
        attention_kernel,
        out_shape=(
            jax.ShapeDtypeStruct((128, BLOCK), bf16),
            jax.ShapeDtypeStruct((2, HALF, 128), f32),
            jax.ShapeDtypeStruct((2, HALF, 256), f32),
            jax.ShapeDtypeStruct((OWN, 64, 512), bf16),
        ),
        in_specs=[VMEM] * 4 + [ANY],
        out_specs=(VMEM, VMEM, VMEM, ANY),
        scratch_shapes=[
            pltpu.VMEM((16, HALF, 256), bf16),
            pltpu.VMEM((2, HALF, 128), bf16),
            pltpu.VMEM((2, HALF, 128), bf16),
            pltpu.VMEM((2, 2, HALF, 128), bf16),
            pltpu.VMEM((2, 2, HALF, 128), bf16),
            pltpu.VMEM((2, 2, 1, HALF), f32),
            pltpu.VMEM((2, 2, 1, HALF), f32),
            pltpu.VMEM((2, 2, 64, HALF), f32),
            pltpu.VMEM((2, 2, 1, HALF), f32),
            pltpu.VMEM((2, 2, 1, HALF), f32),
            pltpu.VMEM((2, 2, 64, HALF), f32),
            pltpu.VMEM((HALF, 256), f32),
            pltpu.VMEM((16, HALF, 256), bf16),
            pltpu.VMEM((8, 2, HALF, 256), bf16),
            pltpu.VMEM((2, 2, HALF, 256), bf16),
            pltpu.VMEM((2, 128, HALF), bf16),
            pltpu.VMEM((128, HALF), bf16),
            pltpu.VMEM((2, 128, HALF), bf16),
            pltpu.VMEM((128, HALF), bf16),
            DMA((8, 2)),
            DMA((16,)),
            DMA((16,)),
            DMA((8, 2)),
            DMA((2, 2)),
            DMA((2, 2)),
            DMA((2, 2)),
            DMA((2, SEQ)),
            DMA((2, SEQ)),
            DMA((4,)),
            DMA((4,)),
            DMA((2,)),
        ],
        compiler_params=pltpu.CompilerParams(
            collective_id=1, has_side_effects=True, vmem_limit_bytes=48 * 1024 * 1024
        ),
        name="attention_both_ways",
    )(q, do, kv, mask, we)


def scatter_kernel(
    o, h, gj, gd, gv, ge, gs, O, H, RJ, RD, RV, RE, RS, other, sums, halves, ends, ss, sr, hs, hr, es, er, ps, pr, loc
):
    dp, g, s = place()
    me = dp * BLK + g
    right, left, across, sibling = ring(s)
    core = s % 2
    barrier = pltpu.get_barrier_semaphore()
    for target in (right, left, sibling):
        pl.semaphore_signal(barrier, inc=1, device_id=(dp, g, target), device_id_type=MESH)

    def greet_peer(t):
        p = (me + t) % OWN
        pl.semaphore_signal(
            barrier, inc=1, device_id=(p // BLK, p % BLK, s), device_id_type=MESH
        )

    loop(1, OWN, greet_peer)
    pl.semaphore_wait(barrier, 3 + OWN - 1)

    parts = (o, h)

    def to_sibling(a, j):
        piece = 2 * ((s // 2 + j) % 4) + 1 - core
        return remote(
            parts[a].at[piece], other.at[a, j], ss.at[a, j], sr.at[a, j], (dp, g, sibling)
        )

    def across_copies():
        return (
            remote(sums.at[0, 2], halves.at[0], hs.at[0], hr.at[0], (dp, g, right)),
            remote(sums.at[1, 2], halves.at[1], hs.at[1], hr.at[1], (dp, g, left)),
        )

    def end_copies(j):
        target = right if j == 1 else left
        return tuple(
            remote(sums.at[a, j], ends.at[a, j // 2], es.at[a, j // 2], er.at[a, j // 2], (dp, g, target))
            for a in range(2)
        )

    def grad_copies(t):
        p = (me + t) % OWN
        target = (p // BLK, p % BLK, s)
        shard = p // BLK * SEQ + (p % BLK - s + SEQ) % SEQ
        return (
            remote(gj.at[shard], RJ.at[me], ps.at[0, t], pr.at[0, me], target),
            remote(gd.at[p], RD.at[me], ps.at[1, t], pr.at[1, me], target),
            remote(gv.at[shard], RV.at[me], ps.at[2, t], pr.at[2, me], target),
            remote(ge.at[shard], RE.at[me], ps.at[3, t], pr.at[3, me], target),
            remote(gs.at[p], RS.at[me], ps.at[4, t], pr.at[4, me], target),
        )

    def start_grads(t):
        for copy in grad_copies(t):
            copy.start()

    shard = dp * SEQ + (g - s + SEQ) % SEQ
    local = (
        pltpu.make_async_copy(gj.at[shard], RJ.at[me], loc.at[0]),
        pltpu.make_async_copy(gd.at[me], RD.at[me], loc.at[1]),
        pltpu.make_async_copy(gv.at[shard], RV.at[me], loc.at[2]),
        pltpu.make_async_copy(ge.at[shard], RE.at[me], loc.at[3]),
        pltpu.make_async_copy(gs.at[me], RS.at[me], loc.at[4]),
    )
    for j in (2, 1, 3, 0):
        for a in range(2):
            to_sibling(a, j).start()
    loop(1, OWN, start_grads)
    for copy in local:
        copy.start()

    def pair_sum(a, j):
        to_sibling(a, j).wait_recv()
        piece = 2 * ((s // 2 + j) % 4) + core
        return parts[a][piece].astype(f32) + other[a, j].astype(f32)

    halfway = across_copies()
    for a in range(2):
        sums[a, 2] = pair_sum(a, 2).astype(bf16)
        halfway[a].start()
    sums[1, 1] = pair_sum(1, 1).astype(bf16)
    sums[0, 3] = pair_sum(0, 3).astype(bf16)
    end_copies(1)[1].start()
    end_copies(3)[0].start()
    halfway[0].wait_recv()
    sums[0, 1] = (pair_sum(0, 1) + halves[0].astype(f32)).astype(bf16)
    end_copies(1)[0].start()
    halfway[1].wait_recv()
    sums[1, 3] = (pair_sum(1, 3) + halves[1].astype(f32)).astype(bf16)
    end_copies(3)[1].start()
    for a, result in ((0, O), (1, H)):
        own = pair_sum(a, 0)
        end_copies(1)[a].wait_recv()
        own = own + ends[a, 0].astype(f32)
        end_copies(3)[a].wait_recv()
        result[...] = own + ends[a, 1].astype(f32)

    for copy in local:
        copy.wait()

    def take_grads(t):
        p = (me + t) % OWN
        target = (p // BLK, p % BLK, s)
        remote(gj.at[0], RJ.at[p], ps.at[0, t], pr.at[0, p], target).wait_recv()
        remote(gd.at[0], RD.at[p], ps.at[1, t], pr.at[1, p], target).wait_recv()
        remote(gv.at[0], RV.at[p], ps.at[2, t], pr.at[2, p], target).wait_recv()
        remote(ge.at[0], RE.at[p], ps.at[3, t], pr.at[3, p], target).wait_recv()
        remote(gs.at[0], RS.at[p], ps.at[4, t], pr.at[4, p], target).wait_recv()
        for copy in grad_copies(t):
            copy.wait_send()

    loop(1, OWN, take_grads)
    for j in range(4):
        for a in range(2):
            to_sibling(a, j).wait_send()
    for copy in halfway + end_copies(1) + end_copies(3):
        copy.wait_send()


def scatter(o, h, gj, gd, gv, ge, gs):
    piece = jax.ShapeDtypeStruct((ROWS, D), f32)
    return pl.pallas_call(
        scatter_kernel,
        out_shape=(piece, piece)
        + tuple(jax.ShapeDtypeStruct(a.shape, a.dtype) for a in (gj, gd, gv, ge, gs)),
        in_specs=[VMEM] * 2 + [ANY] * 5,
        out_specs=(VMEM, VMEM) + (ANY,) * 5,
        scratch_shapes=[
            pltpu.VMEM((2, 4, ROWS, D), bf16),
            pltpu.VMEM((2, 4, ROWS, D), bf16),
            pltpu.VMEM((2, ROWS, D), bf16),
            pltpu.VMEM((2, 2, ROWS, D), bf16),
            DMA((2, 4)),
            DMA((2, 4)),
            DMA((2,)),
            DMA((2,)),
            DMA((2, 2)),
            DMA((2, 2)),
            DMA((5, OWN)),
            DMA((5, OWN)),
            DMA((5,)),
        ],
        compiler_params=pltpu.CompilerParams(
            collective_id=2, has_side_effects=True, vmem_limit_bytes=40 * 1024 * 1024
        ),
        name="scatter_sums",
    )(o, h, gj, gd, gv, ge, gs)


def spread_kernel(rj, re, rv, rs, rd, FJ, FE, FV, FS, FD, as_, ar, bs, br, loc):
    dp, g, s = place()
    owner = (g - s + SEQ) % SEQ
    own = jnp.where(owner == s, 1, 0)
    barrier = pltpu.get_barrier_semaphore()

    def source(t):
        k = (s + t) % SEQ
        return (dp, (s + k) % BLK, k), k

    def greet(t):
        @pl.when(jnp.logical_or(t > 0, own == 0))
        def _():
            pl.semaphore_signal(barrier, inc=1, device_id=source(t)[0], device_id_type=MESH)

        @pl.when(t > 0)
        def _():
            pl.semaphore_signal(
                barrier, inc=1, device_id=(dp, (g + t) % BLK, s), device_id_type=MESH
            )

    loop(0, 8, greet)
    pl.semaphore_wait(barrier, 8 - own + 7)

    def row_copies(t):
        target = (dp, (g + t) % BLK, owner)
        return (
            remote(rj, FJ.at[s], as_.at[0, t], ar.at[0, s], target),
            remote(re, FE.at[s], as_.at[1, t], ar.at[1, s], target),
            remote(rv, FV.at[s], as_.at[2, t], ar.at[2, s], target),
        )

    def column_copies(t):
        target = (dp, (g + t) % BLK, s)
        return (
            remote(rs, FS.at[g], bs.at[0, t], br.at[0, g], target),
            remote(rd, FD.at[g], bs.at[1, t], br.at[1, g], target),
        )

    local_rows = (
        pltpu.make_async_copy(rj, FJ.at[s], loc.at[0]),
        pltpu.make_async_copy(re, FE.at[s], loc.at[1]),
        pltpu.make_async_copy(rv, FV.at[s], loc.at[2]),
    )
    local = (
        pltpu.make_async_copy(rs, FS.at[g], loc.at[3]),
        pltpu.make_async_copy(rd, FD.at[g], loc.at[4]),
    )

    def start(t):
        @pl.when(jnp.logical_or(t > 0, own == 0))
        def _():
            for copy in row_copies(t):
                copy.start()

        @pl.when(t > 0)
        def _():
            for copy in column_copies(t):
                copy.start()

    loop(0, 8, start)
    for copy in local:
        copy.start()

    @pl.when(own == 1)
    def _():
        for copy in local_rows:
            copy.start()
        for copy in local_rows:
            copy.wait()

    for copy in local:
        copy.wait()

    def take(t):
        @pl.when(jnp.logical_or(t > 0, own == 0))
        def _():
            target, k = source(t)
            remote(rj, FJ.at[k], as_.at[0, t], ar.at[0, k], target).wait_recv()
            remote(re, FE.at[k], as_.at[1, t], ar.at[1, k], target).wait_recv()
            remote(rv, FV.at[k], as_.at[2, t], ar.at[2, k], target).wait_recv()
            for copy in row_copies(t):
                copy.wait_send()

        @pl.when(t > 0)
        def _():
            k = (g + t) % BLK
            target = (dp, k, s)
            remote(rs, FS.at[k], bs.at[0, t], br.at[0, k], target).wait_recv()
            remote(rd, FD.at[k], bs.at[1, t], br.at[1, k], target).wait_recv()
            for copy in column_copies(t):
                copy.wait_send()

    loop(0, 8, take)


def spread(*parts):
    return pl.pallas_call(
        spread_kernel,
        out_shape=tuple(jax.ShapeDtypeStruct((8,) + a.shape, a.dtype) for a in parts),
        in_specs=[ANY] * 5,
        out_specs=(ANY,) * 5,
        scratch_shapes=[DMA((3, 8)), DMA((3, 8)), DMA((2, 8)), DMA((2, 8)), DMA((5,))],
        compiler_params=pltpu.CompilerParams(collective_id=3, has_side_effects=True),
        name="spread_gradients",
    )(*parts)


def rotary_tables(positions):
    half_dims = ROT // 2
    freqs = jnp.power(10000.0, -2.0 * jnp.arange(half_dims).astype(f32) / ROT)
    angles = positions.astype(f32)[:, None] * jnp.tile(freqs, 128 // half_dims)[None, :]
    dim = (jnp.arange(128) % HEAD_DIM)[None, :]
    own = jnp.where(dim < ROT, jnp.cos(angles), 1.0)
    swapped = jnp.where(dim < half_dims, -jnp.sin(angles), jnp.sin(angles))
    return own, jnp.where(dim < ROT, swapped, 0.0)


def exchange():
    half_dims = ROT // 2
    lane = jnp.arange(128)
    dim = lane % HEAD_DIM
    source = jnp.where(dim < half_dims, lane + half_dims, lane - half_dims)
    return ((lane[:, None] == source[None, :]) & (dim < ROT)[None, :]).astype(f32)


def rotate(rows, own, swapped):
    other = jnp.dot(
        rows, exchange().astype(rows.dtype), precision=lax.Precision.HIGHEST,
        preferred_element_type=f32,
    )
    return rows.astype(f32) * own + other * swapped


def adam_update(grad_in, first_old, second_old, master, rate, decay_rate):
    first_new = beta_one * first_old + (1.0 - beta_one) * grad_in
    second_new = beta_two * second_old + (1.0 - beta_two) * grad_in * grad_in
    root_second = jnp.sqrt(second_new / (1.0 - beta_two**STEP)) + adam_eps
    master_new = (
        master * (1.0 - rate * decay_rate)
        - rate * (first_new / (1.0 - beta_one**STEP)) / root_second
    )
    return (first_new, second_new, master_new)


def norm_stats(source):
    centred = source - jnp.mean(source, axis=-1, keepdims=True)
    inv_std = lax.rsqrt(jnp.mean(centred * centred, axis=-1, keepdims=True) + eps_norm)
    return centred * inv_std, inv_std


def shards(
    inputs,
    cotangent,
    joint_weight,
    joint_first,
    joint_second,
    dense_weight,
    dense_first,
    dense_second,
    expand_weight,
    expand_first,
    expand_second,
    shrink_weight,
    shrink_first,
    shrink_second,
    vectors,
    vectors_first,
    vectors_second,
):
    dp, g, s = place()
    wj = joint_weight.astype(bf16).reshape(64, 3, 2, SEQ, 64)
    wj = jnp.transpose(wj, (3, 0, 1, 2, 4)).reshape(SEQ, 64, 384)
    we = expand_weight.astype(bf16).reshape(64, 2, SEQ, 256)
    we = jnp.transpose(we, (2, 0, 1, 3)).reshape(SEQ, 64, 512)
    vec = jnp.concatenate([vectors[:, :9].T.reshape(576), vectors[:, 9:].reshape(256)])
    vec = jnp.pad(vec.astype(bf16), (0, 2048 - 832)).reshape(16, 128)
    X, C, WJ, WE, WS, WD, VEC = gather(
        inputs, cotangent, wj, we, shrink_weight.astype(bf16), dense_weight.astype(bf16), vec
    )
    X = X.reshape(BLOCK, D)
    C = C.reshape(BLOCK, D)
    WJ = WJ.reshape(D, 384)
    WS = WS.reshape(512, D)
    WD = WD.reshape(128, D)
    VEC = VEC.reshape(OWN, 2048).astype(f32)
    table = jnp.swapaxes(VEC[:, :576].reshape(OWN, 9, 64), 0, 1).reshape(9, D)
    gain_one, shift_one, gain_two, shift_two = (table[i] for i in range(4))
    bias_joint = jnp.take(table[4:7].reshape(3, 2, SEQ, 64), s, axis=2).reshape(384)
    bias_out = table[7] + table[8]
    bias_expand = jnp.take(VEC[:, 576:832].reshape(2, SEQ, 256), s, axis=1).reshape(512)

    hat, _ = norm_stats(X.astype(f32))
    normed_one = (hat * gain_one + shift_one).astype(bf16)
    normed_two = (hat * gain_two + shift_two).astype(bf16)
    triple = (jnp.dot(normed_one, WJ, preferred_element_type=f32) + bias_joint).astype(bf16)
    positions = g * BLOCK + jnp.arange(BLOCK)
    cosine, sine = rotary_tables(positions)
    queries = rotate(triple[:, 0:128], cosine, sine).astype(bf16)
    keys = rotate(triple[:, 128:256], cosine, sine).astype(bf16)
    kv = jnp.concatenate([keys, triple[:, 256:]], axis=1).reshape(2, HALF, 256)
    grad_att = lax.dot_general(C, WD, NT, preferred_element_type=f32).astype(bf16)

    scaled = (queries.astype(f32) * HEAD_DIM ** (-0.5)).astype(bf16)
    lane = jnp.arange(128)
    mask = jnp.stack([lane < 64, lane >= 64]).astype(bf16).reshape(2, 1, 128)
    att, dq, dkv, WE = attention(
        scaled.reshape(2, HALF, 128),
        grad_att.reshape(2, HALF, 128),
        kv,
        mask,
        WE,
    )
    WE = WE.reshape(D, 512)

    expand_pre = jnp.dot(normed_two, WE, preferred_element_type=f32) + bias_expand
    activated, gelu_pull = jax.vjp(partial(jax.nn.gelu, approximate=False), expand_pre)
    activated = activated.astype(bf16)
    mlp_part = jnp.dot(activated, WS, preferred_element_type=f32)
    grad_act = lax.dot_general(C, WS, NT, preferred_element_type=f32)
    grad_pre = gelu_pull(grad_act)[0].astype(bf16)
    grad_shrink = jnp.dot(activated.T, C, preferred_element_type=f32).astype(bf16)
    grad_expand = jnp.dot(normed_two.T, grad_pre, preferred_element_type=f32).astype(bf16)

    grad_normed_two = lax.dot_general(grad_pre, WE, NT, preferred_element_type=f32)
    out_part = lax.dot_general(att, WD, (((0,), (0,)), ((), ())), preferred_element_type=f32)
    out_part = (out_part + mlp_part).astype(bf16)
    grad_dense = jnp.dot(att, C, preferred_element_type=f32).astype(bf16)
    grad_q = rotate(dq.reshape(BLOCK, 128), cosine, -sine)
    dkv = dkv.reshape(BLOCK, 256)
    grad_k = rotate(dkv[:, :128], cosine, -sine)
    grad_triple = jnp.concatenate([grad_q, grad_k, dkv[:, 128:]], axis=1).astype(bf16)
    grad_joint = jnp.dot(normed_one.T, grad_triple, preferred_element_type=f32).astype(bf16)
    grad_normed_one = lax.dot_general(grad_triple, WJ, NT, preferred_element_type=f32)
    grad_hat = (grad_normed_one * gain_one + grad_normed_two * gain_two).astype(bf16)

    first = jnp.where(s == 0, 1.0, 0.0)
    grad_bias_out = first * jnp.sum(C.astype(f32), axis=0)
    mine = (jnp.arange(SEQ) == s).astype(f32)
    grad_bias_joint = jnp.sum(grad_triple.astype(f32), axis=0).reshape(3, 2, 1, 64)
    grad_bias_joint = (grad_bias_joint * mine[None, None, :, None]).reshape(3, D)
    grad_bias_expand = jnp.sum(grad_pre.astype(f32), axis=0).reshape(2, 1, 256)
    grad_bias_expand = (grad_bias_expand * mine[None, :, None]).reshape(OWN, 256)
    grad_rows = jnp.concatenate(
        [
            jnp.sum(grad_normed_one * hat, axis=0)[None],
            jnp.sum(grad_normed_one, axis=0)[None],
            jnp.sum(grad_normed_two * hat, axis=0)[None],
            jnp.sum(grad_normed_two, axis=0)[None],
            grad_bias_joint,
            grad_bias_out[None],
            grad_bias_out[None],
        ]
    )
    grad_rows = jnp.swapaxes(grad_rows.reshape(9, OWN, 64), 0, 1).reshape(OWN, 576)
    gv = jnp.pad(jnp.concatenate([grad_rows, grad_bias_expand], axis=1), ((0, 0), (0, 192)))
    gd = jnp.transpose(grad_dense.reshape(2, 64, BLK, 128), (0, 2, 1, 3)).reshape(OWN, 64, 128)

    O, H, RJ, RD, RV, RE, RS = scatter(
        out_part.reshape(8, ROWS, D),
        grad_hat.reshape(8, ROWS, D),
        grad_joint.reshape(OWN, 64, 384),
        gd,
        gv.reshape(OWN, 8, 128),
        grad_expand.reshape(OWN, 64, 512),
        grad_shrink.reshape(OWN, 32, D),
    )

    def total(parts):
        return jnp.sum(parts.astype(f32), axis=0)

    FJ, FE, FV, FS, FD = spread(
        total(RJ).astype(bf16),
        total(RE).astype(bf16),
        total(RV),
        total(RS).astype(bf16),
        total(RD).astype(bf16),
    )

    source = inputs.astype(f32)
    output = (source + O + bias_out).astype(bf16)
    own_hat, own_inv = norm_stats(source)
    own_grad = H
    input_grad = cotangent.astype(f32) + own_inv * (
        own_grad
        - jnp.mean(own_grad, axis=-1, keepdims=True)
        - own_hat * jnp.mean(own_grad * own_hat, axis=-1, keepdims=True)
    )

    total_joint = jnp.transpose(FJ.reshape(SEQ, 64, 3, 2, 64), (1, 2, 3, 0, 4)).reshape(64, 3 * D)
    total_expand = jnp.transpose(FE.reshape(SEQ, 64, 2, 256), (1, 2, 0, 3)).reshape(64, FF)
    total_shrink = FS.reshape(256, D)
    total_dense = jnp.transpose(FD, (1, 0, 2)).reshape(64, D)
    sums = jnp.sum(FV, axis=0).reshape(1024)
    total_vectors = jnp.concatenate(
        [sums[:576].reshape(9, 64).T, sums[576:832].reshape(64, 4)], axis=1
    )
    joint = adam_update(
        total_joint.astype(f32), joint_first, joint_second, joint_weight, 0.1, weight_decay
    )
    dense = adam_update(
        total_dense.astype(f32), dense_first, dense_second, dense_weight, 1.0, weight_decay
    )
    expand = adam_update(
        total_expand.astype(f32), expand_first, expand_second, expand_weight, 0.1, weight_decay
    )
    shrink = adam_update(
        total_shrink.astype(f32), shrink_first, shrink_second, shrink_weight, 0.05, weight_decay
    )
    vector = adam_update(total_vectors, vectors_first, vectors_second, vectors, 1.0, 0.0)
    return (output, input_grad) + joint + dense + expand + shrink + vector


def solution(mesh):
    return jax.shard_map(
        shards,
        mesh=mesh,
        in_specs=(
            P(("dp", "blk", "seq"), None),
            P(("dp", "blk", "seq"), None),
            P(("dp", "seq"), None),
            P(("dp", "seq"), None),
            P(("dp", "seq"), None),
            P(("dp", "seq"), None),
            P(("dp", "seq"), None),
            P(("dp", "seq"), None),
            P(("dp", "seq"), None),
            P(("dp", "seq"), None),
            P(("dp", "seq"), None),
            P(("dp", "seq"), None),
            P(("dp", "seq"), None),
            P(("dp", "seq"), None),
            P(("dp", "seq"), None),
            P(("dp", "seq"), None),
            P(("dp", "seq"), None),
        ),
        out_specs=(
            P(("dp", "blk", "seq"), None),
            P(("dp", "blk", "seq"), None),
            P(("dp", "seq"), None),
            P(("dp", "seq"), None),
            P(("dp", "seq"), None),
            P(("dp", "seq"), None),
            P(("dp", "seq"), None),
            P(("dp", "seq"), None),
            P(("dp", "seq"), None),
            P(("dp", "seq"), None),
            P(("dp", "seq"), None),
            P(("dp", "seq"), None),
            P(("dp", "seq"), None),
            P(("dp", "seq"), None),
            P(("dp", "seq"), None),
            P(("dp", "seq"), None),
            P(("dp", "seq"), None),
        ),
        check_vma=False,
    )
```
